256 devices in a mesh: ctx: 32 (over x, z), head: 8 (over y, core).
Axes of the slice: x: 4, y: 4, z: 8, core: 2. Of those that a mesh axis runs over, the one named last changes fastest.
Arguments:
- queries: bfloat16 [32768, 4096], P(('ctx', 'head')), may hold values from -6 to 6
- key_rows: bfloat16 [32768, 4096], P(('ctx', 'head')), may hold values from -6 to 6
- value_rows: bfloat16 [32768, 4096], P(('ctx', 'head')), may hold values from -6 to 6
- out_grad: bfloat16 [32768, 4096], P(('ctx', 'head')), may hold values from -6 to 6
Outputs:
- attended: bfloat16 [32768, 4096], P('ctx', 'head')
- query_grad: bfloat16 [32768, 4096], P('ctx', 'head')
- key_grad: bfloat16 [32768, 4096], P('ctx', 'head')
- value_grad: bfloat16 [32768, 4096], P('ctx', 'head')
The draws below stay inside these ranges and needn't reach their ends.
All inputs are finite; a program needn't handle non-finite values.
Results may differ from the reference program's by a relative error of at most 0.0049.
Values may be sent and summed in bfloat16 or wider, within the bound.
A program may use at most 128 MiB of HBM per device.

```python
import math
import jax
import jax.numpy as jnp
from jax import lax

HEADS = 32
HD = 128
TOK_DEV = 1024
TOKENS = 32768
WIDTH = 4096
N_CTX = 32


def level_of(stream_key, dims, pieces, low, high):
    def one(position, parts):
        steps = jax.random.uniform(jax.random.fold_in(jax.random.fold_in(stream_key, 6), position), (parts,), jnp.float32, low / len(pieces), high / len(pieces))
        return jnp.repeat(jnp.exp(steps), dims[position] // parts).reshape((-1,) + (1,) * (len(dims) - position - 1))

    level = one(*pieces[0])
    for cut in pieces[1:]:
        level = level * one(*cut)
    return level


def noise(own_key, extent, scale, reach, shards=(), dtype=jnp.bfloat16):
    values = scale * jax.random.normal(own_key, extent, jnp.float32)
    if shards:
        values = values * level_of(own_key, extent, shards, -0.22, 0.18)
    return jnp.clip(values, -reach, reach).astype(dtype)


def setup_inputs(seed: int = 0) -> dict:
    key_of = jax.random.split(jax.random.key(seed), 5)
    return {
        "queries": noise(key_of[0], (TOKENS, WIDTH), 1.0, 6.0, ((0, 256),)),
        "key_rows": noise(key_of[1], (TOKENS, WIDTH), 1.0, 6.0, ((0, 256),)),
        "value_rows": noise(key_of[2], (TOKENS, WIDTH), 1.0, 6.0, ((0, 256),)),
        "out_grad": noise(key_of[3], (TOKENS, WIDTH), 1.0, 6.0, ((0, 256),)),
    }


def block_pass(items):
    query_blk, key_blk, value_blk, grad_blk, prefix_b, suffix_b = items
    scale = 1.0 / math.sqrt(HD * TOKENS)
    count = query_blk.shape[0]
    causal = lax.broadcasted_iota(jnp.int32, (count, count), 0) >= lax.broadcasted_iota(jnp.int32, (count, count), 1)
    scores = jnp.dot(query_blk, key_blk.T, preferred_element_type=jnp.float32)
    attn_b = jnp.where(causal, scores * scale, 0.0).astype(jnp.bfloat16)
    grads = jnp.dot(grad_blk, value_blk.T, preferred_element_type=jnp.float32)
    back_b = jnp.where(causal, grads * scale, 0.0).astype(jnp.bfloat16)
    output = jnp.dot(attn_b, value_blk, preferred_element_type=jnp.float32) + jnp.dot(query_blk, prefix_b, preferred_element_type=jnp.float32)
    dquery = jnp.dot(back_b, key_blk, preferred_element_type=jnp.float32) + jnp.dot(grad_blk, prefix_b.T, preferred_element_type=jnp.float32)
    dkey = jnp.dot(back_b.T, query_blk, preferred_element_type=jnp.float32) + jnp.dot(value_blk, suffix_b.T, preferred_element_type=jnp.float32)
    dvalue = jnp.dot(attn_b.T, grad_blk, preferred_element_type=jnp.float32) + jnp.dot(key_blk, suffix_b, preferred_element_type=jnp.float32)
    return (output.astype(jnp.bfloat16), dquery.astype(jnp.bfloat16), dkey.astype(jnp.bfloat16), dvalue.astype(jnp.bfloat16))

def head_pass(items):
    query_h, key_h, value_h, grad_h = items
    scale = 1.0 / math.sqrt(HD * TOKENS)
    kv_states = jnp.einsum('nld,nle->nde', key_h.astype(jnp.float32), value_h.astype(jnp.float32))
    qg_states = jnp.einsum('nld,nle->nde', query_h.astype(jnp.float32), grad_h.astype(jnp.float32))
    prefix = jnp.cumsum(kv_states, axis=0) - kv_states
    suffix = lax.optimization_barrier(jnp.sum(qg_states, axis=0))[None] - jnp.cumsum(qg_states, axis=0)
    prefix_b = (scale * prefix).astype(jnp.bfloat16)
    suffix_b = (scale * suffix).astype(jnp.bfloat16)
    return lax.map(block_pass, (query_h, key_h, value_h, grad_h, prefix_b, suffix_b))

def reference(queries, key_rows, value_rows, out_grad):

    def split(array):
        return jnp.moveaxis(array.reshape(N_CTX, TOK_DEV, HEADS, HD), 2, 0)
    results = lax.map(head_pass, (split(queries), split(key_rows), split(value_rows), split(out_grad)))

    def join(array):
        return jnp.moveaxis(array, 0, 2).reshape(TOKENS, HEADS * HD)
    return (join(results[0]), join(results[1]), join(results[2]), join(results[3]))
```

```python
import math

import jax
import jax.numpy as jnp
from jax import lax
from jax.experimental import pallas as pl
from jax.experimental.pallas import tpu as pltpu
from jax.sharding import PartitionSpec as P

HD = 128
NX, NZ, NY = 4, 8, 4
SUB = 256
MESH = pl.DeviceIdType.MESH
F32 = jnp.float32
BF16 = jnp.bfloat16
HOPS = (1, 3, 2)


def mm(left, right, left_dim, right_dim):
    return lax.dot_general(
        left, right, (((left_dim,), (right_dim,)), ((), ())), preferred_element_type=F32
    )


def kernel(
    scale, q, k, v, g, o0, o1, o2, o3,
    recv, own, acc, sib_out, sib_in, early_out, early, subs, states, pin, totals, pout, entering,
    at_sub, raw_send, raw_recv, own_sem, sib_send, sib_recv, early_send, early_recv,
    scan_send, scan_recv, up_sem,
):
    inputs = (q, k, v, g)
    outputs = (o0, o1, o2, o3)
    ctx = lax.axis_index("ctx")
    head = lax.axis_index("head")
    x, z = ctx // NZ, ctx % NZ
    y, core = head // 2, head % 2
    sibling = y * 2 + (1 - core)

    barrier = pltpu.get_barrier_semaphore()
    for d in range(1, 8):
        pl.semaphore_signal(barrier, inc=1, device_id=(ctx, (head + d) % 8), device_id_type=MESH)
    for d in range(1, NX):
        pl.semaphore_signal(barrier, inc=1, device_id=((x + d) % NX * NZ + z, head), device_id_type=MESH)

    def greet(later, carry):
        pl.semaphore_signal(barrier, inc=1, device_id=(x * NZ + later, head), device_id_type=MESH)
        return carry

    lax.fori_loop(z + 1, NZ, greet, 0)
    for a in range(4):
        pltpu.make_async_copy(inputs[a], own.at[a], own_sem).start()
    pl.semaphore_wait(barrier, 7 + NX - 1 + z)

    def answer(earlier, carry):
        pl.semaphore_signal(up_sem, inc=1, device_id=(x * NZ + earlier, head), device_id_type=MESH)
        return carry

    lax.fori_loop(0, z, answer, 0)

    def raw(h, dy, dc, a):
        to = (y + dy) % NY * 2 + (core + dc) % 2
        pltpu.make_async_remote_copy(
            src_ref=inputs[a].at[:, pl.ds(pl.multiple_of(to * 512 + h * HD, HD), HD)],
            dst_ref=recv.at[a, h, pl.ds(pl.multiple_of(head * HD, HD), HD), :],
            send_sem=raw_send,
            recv_sem=raw_recv.at[h, (NY - dy) % NY],
            device_id=(ctx, to),
            device_id_type=MESH,
        ).start()

    def send_head(h):
        for a in range(4):
            pltpu.make_async_copy(
                inputs[a].at[:, pl.ds(pl.multiple_of(head * 512 + h * HD, HD), HD)],
                recv.at[a, h, pl.ds(pl.multiple_of(head * HD, HD), HD), :],
                raw_recv.at[h, 0],
            ).start()
            raw(h, 0, 1, a)
        for dy in HOPS:
            for dc in range(2):
                for a in range(4):
                    raw(h, dy, dc, a)

    send_head(0)

    for a in range(4):
        pltpu.make_async_copy(inputs[a], own.at[a], own_sem).wait()

    def partial(dest, st):
        cols = pl.ds(pl.multiple_of(dest * 512 + 256 + st // 2 * HD, HD), HD)
        if st % 2 == 0:
            return mm(own[1, :, cols], own[2, :, cols], 0, 0)
        return mm(own[0, :, cols], own[3, :, cols], 0, 0)

    for n, dy in enumerate(HOPS + (0,)):
        to_y = (y + dy) % NY
        for st in range(4):
            sib_out[n, st] = partial(to_y * 2 + 1 - core, st)
        pltpu.make_async_remote_copy(
            src_ref=sib_out.at[n],
            dst_ref=sib_in.at[n],
            send_sem=sib_send,
            recv_sem=sib_recv.at[n],
            device_id=(ctx, sibling),
            device_id_type=MESH,
        ).start()
    for n, dy in enumerate(HOPS + (0,)):
        pltpu.make_async_copy(sib_in.at[n], sib_in.at[n], sib_recv.at[n]).wait()
        to = (y + dy) % NY * 2 + core
        for st in range(4):
            both = (partial(to, st) + sib_in[n, st]).astype(BF16)
            if dy == 0:
                early[y, st] = both
            else:
                early_out[n, st] = both
        if dy != 0:
            pltpu.make_async_remote_copy(
                src_ref=early_out.at[n],
                dst_ref=early.at[y],
                send_sem=early_send,
                recv_sem=early_recv,
                device_id=(ctx, to),
                device_id_type=MESH,
            ).start()

    def send_rest(h, carry):
        send_head(h)
        return carry

    lax.fori_loop(1, 4, send_rest, 0)

    row = lax.broadcasted_iota(jnp.int32, (SUB, SUB), 0)
    col = lax.broadcasted_iota(jnp.int32, (SUB, SUB), 1)
    causal = row >= col

    def load(h, i):
        return tuple(recv[a, h, pl.ds(pl.multiple_of(i * SUB, SUB), SUB), :] for a in range(4))

    def within(qs, ks, vs, gs):
        attn = jnp.where(causal, mm(qs, ks, 1, 1), 0.0).astype(BF16)
        back = jnp.where(causal, mm(gs, vs, 1, 1), 0.0).astype(BF16)
        return mm(attn, vs, 1, 0), mm(back, ks, 1, 0), mm(back, qs, 0, 0), mm(attn, gs, 0, 0)

    def across(qs, ks, vs, gs, pre, suf):
        return mm(qs, pre, 1, 0), mm(gs, pre, 1, 1), mm(vs, suf, 1, 1), mm(ks, suf, 1, 0)

    def arrive(h, m):
        j = m + m // 2 - 2 * (m // 3)
        i = (y + j) % NY
        landed = recv.at[:, h, pl.ds(pl.multiple_of(i * SUB, SUB), SUB), :]
        pltpu.make_async_copy(landed, landed, raw_recv.at[h, j]).wait()
        return i

    def first_heads(h):
        def one(m, carry):
            i = arrive(h, m)
            parts = load(h, i)
            qs, ks, vs, gs = parts
            subs[i, 2 * h] = mm(ks, vs, 0, 0)
            subs[i, 2 * h + 1] = mm(qs, gs, 0, 0)
            rows = pl.ds(pl.multiple_of(i * SUB, SUB), SUB)
            for n, part in enumerate(within(*parts)):
                acc[n, h, rows, :] = part
            return carry

        lax.fori_loop(0, NY, one, 0)
        for st in (2 * h, 2 * h + 1):
            total = subs[0, st] + subs[1, st] + subs[2, st] + subs[3, st]
            states[1, pl.ds(st * HD, HD), :] = total.astype(BF16)

    def store(h, i, values):
        rows = pl.ds(pl.multiple_of(i * SUB, SUB), SUB)
        for ref, value in zip(outputs, values):
            ref[rows, pl.ds(h * HD, HD)] = (value * scale).astype(BF16)

    def last_heads(h, low, high):
        def one(m, carry):
            i = arrive(h, m)
            parts = load(h, i)
            st = 2 * (h - 2)
            far = across(*parts, at_sub[0, i, st], at_sub[0, i, st + 1])
            store(h, i, [near + more for near, more in zip(within(*parts), far)])
            return carry

        lax.fori_loop(low, high, one, 0)

    def finish(h):
        def one(i, carry):
            rows = pl.ds(pl.multiple_of(i * SUB, SUB), SUB)
            far = across(*load(h, i), at_sub[1, i, 2 * h], at_sub[1, i, 2 * h + 1])
            store(h, i, [acc[n, h, rows, :] + more for n, more in enumerate(far)])
            return carry

        lax.fori_loop(0, NY, one, 0)

    ahead = z % 4 < 2
    far_first = (4, 3, 5, 2, 6, 1, 7)

    def scan_one(n):
        pin[n, z] = states[n, pl.ds(pl.multiple_of(z * 64, 64), 64), :]
        for dz in far_first:
            to = (z + dz) % NZ
            pltpu.make_async_remote_copy(
                src_ref=states.at[n, pl.ds(pl.multiple_of(to * 64, 64), 64), :],
                dst_ref=pin.at[n, z],
                send_sem=scan_send.at[n, 0],
                recv_sem=scan_recv.at[n, 0],
                device_id=(x * NZ + to, head),
                device_id_type=MESH,
            ).start()

    def scan_two(n):
        landed = pin.at[n, pl.ds(0, NZ - 1)]
        pltpu.make_async_copy(landed, landed, scan_recv.at[n, 0]).wait()
        total = pin[n, 0].astype(F32)
        for i in range(1, NZ):
            total = total + pin[n, i].astype(F32)
        totals[n, x] = total
        for dx in (2, 1, 3):
            pltpu.make_async_remote_copy(
                src_ref=totals.at[n, x],
                dst_ref=totals.at[n, x],
                send_sem=scan_send.at[n, 1],
                recv_sem=scan_recv.at[n, 1],
                device_id=((x + dx) % NX * NZ + z, head),
                device_id_type=MESH,
            ).start()

    def scan_three(n):
        landed = totals.at[n, pl.ds(0, NX - 1)]
        pltpu.make_async_copy(landed, landed, scan_recv.at[n, 1]).wait()
        base = jnp.zeros((64, HD), F32)
        for i in range(NX):
            counts = jnp.logical_or(jnp.logical_and(ahead, i < x), jnp.logical_and(jnp.logical_not(ahead), i > x))
            base = base + jnp.where(counts, totals[n, i], 0.0)
        total = totals[n, x]
        before = jnp.zeros((64, HD), F32)
        for i in range(NZ):
            mine = pin[n, i].astype(F32)
            part = jnp.where(ahead, before, total - before - mine)
            pout[n, i] = (base + part).astype(BF16)
            before = before + mine
        entering[n, pl.ds(pl.multiple_of(z * 64, 64), 64), :] = pout[n, z]
        for dz in far_first:
            to = (z + dz) % NZ
            pltpu.make_async_remote_copy(
                src_ref=pout.at[n, to],
                dst_ref=entering.at[n, pl.ds(pl.multiple_of(z * 64, 64), 64), :],
                send_sem=scan_send.at[n, 2],
                recv_sem=scan_recv.at[n, 2],
                device_id=(x * NZ + to, head),
                device_id_type=MESH,
            ).start()

    def scan_end(n):
        landed = pout.at[n, pl.ds(0, NZ - 1)]
        pltpu.make_async_copy(landed, landed, scan_recv.at[n, 2]).wait()
        for st in range(4):
            state = entering[n, pl.ds(st * HD, HD), :].astype(F32)
            for i in range(NY) if st % 2 == 0 else reversed(range(NY)):
                at_sub[n, i, st] = state.astype(BF16)
                sub = early[i, st].astype(F32) if n == 0 else subs[i, st]
                state = state + sub

    first_heads(0)

    landed = early_out.at[pl.ds(0, 3)]
    pltpu.make_async_copy(landed, landed, early_recv).wait()
    for st in range(4):
        total = early[0, st].astype(F32)
        for i in range(1, NY):
            total = total + early[i, st].astype(F32)
        states[0, pl.ds(st * HD, HD), :] = total.astype(BF16)

    @pl.when(z < NZ - 1)
    def _():
        pl.semaphore_wait(up_sem, NZ - 1 - z)

    scan_one(0)

    first_heads(1)
    scan_one(1)
    scan_two(0)
    scan_three(0)
    scan_two(1)
    scan_three(1)
    scan_end(0)
    last_heads(2, 0, 4)
    last_heads(3, 0, 3)
    scan_end(1)
    finish(0)
    finish(1)
    last_heads(3, 3, 4)

    sent = recv.at[:, :, pl.ds(0, 896), :]
    pltpu.make_async_copy(sent, sent, raw_send).wait()
    pltpu.make_async_copy(sib_out, sib_out, sib_send).wait()
    sent = early_out.at[pl.ds(0, 3)]
    pltpu.make_async_copy(sent, sent, early_send).wait()
    for n in range(2):
        sent = pout.at[n, pl.ds(0, NZ - 1)]
        pltpu.make_async_copy(sent, sent, scan_send.at[n, 0]).wait()
        pltpu.make_async_copy(sent, sent, scan_send.at[n, 2]).wait()
        sent = totals.at[n, pl.ds(0, NX - 1)]
        pltpu.make_async_copy(sent, sent, scan_send.at[n, 1]).wait()


def on_device(queries, key_rows, value_rows, out_grad):
    def body(*refs):
        kernel(1.0 / math.sqrt(4194304), *refs)

    dma = pltpu.SemaphoreType.DMA
    return pl.pallas_call(
        body,
        out_shape=[pltpu.VMEM((1024, 512), BF16)] * 4,
        in_specs=[pl.BlockSpec(memory_space=pl.ANY)] * 4,
        out_specs=[pl.BlockSpec(memory_space=pltpu.VMEM)] * 4,
        scratch_shapes=[
            pltpu.VMEM((4, 4, 1024, HD), BF16),
            pltpu.VMEM((4, 128, 4096), BF16),
            pltpu.VMEM((4, 2, 1024, HD), F32),
            pltpu.VMEM((4, 4, HD, HD), F32),
            pltpu.VMEM((4, 4, HD, HD), F32),
            pltpu.VMEM((4, 4, HD, HD), BF16),
            pltpu.VMEM((4, 4, HD, HD), BF16),
            pltpu.VMEM((4, 4, HD, HD), F32),
            pltpu.VMEM((2, 512, HD), BF16),
            pltpu.VMEM((2, NZ, 64, HD), BF16),
            pltpu.VMEM((2, NX, 64, HD), F32),
            pltpu.VMEM((2, NZ, 64, HD), BF16),
            pltpu.VMEM((2, 512, HD), BF16),
            pltpu.VMEM((2, 4, 4, HD, HD), BF16),
            dma,
            dma((4, 4)),
            dma,
            dma,
            dma((4,)),
            dma,
            dma,
            dma((2, 3)),
            dma((2, 3)),
            pltpu.SemaphoreType.REGULAR,
        ],
        compiler_params=pltpu.CompilerParams(
            collective_id=0, has_side_effects=True, vmem_limit_bytes=58 * 2**20
        ),
        name="linear_attention",
    )(queries, key_rows, value_rows, out_grad)


def solution(mesh):
    return jax.shard_map(
        on_device,
        mesh=mesh,
        in_specs=(P(("ctx", "head"), None),) * 4,
        out_specs=(P("ctx", "head"),) * 4,
        check_vma=False,
    )
```

```python
import math

import jax
import jax.numpy as jnp
from jax import lax
from jax.experimental import pallas as pl
from jax.experimental.pallas import tpu as pltpu
from jax.sharding import PartitionSpec as P

HD = 128
NX, NZ, NY = 4, 8, 4
SUB = 256
SLICE = 2 * HD // NZ
VMEM_LIMIT = 58 * 2**20
MESH = pl.DeviceIdType.MESH
F32 = jnp.float32
BF16 = jnp.bfloat16


def mm(left, right, left_dim, right_dim):
    return lax.dot_general(
        left, right, (((left_dim,), (right_dim,)), ((), ())), preferred_element_type=F32
    )


def kernel(
    scale, q, k, v, g, o0, o1, o2, o3,
    recv, own, acc, sib_out, sib_in, early_out, early_in, onward, subs, states, pin, totals, pout,
    entering, inner, raw_send, raw_recv, own_sem, sib_send, sib_recv, early_send, early_recv,
    scan_send, scan_recv, up_sem,
):
    inputs = (q, k, v, g)
    outputs = (o0, o1, o2, o3)
    ctx = lax.axis_index("ctx")
    head = lax.axis_index("head")
    x, z = ctx // NZ, ctx % NZ
    y, core = head // 2, head % 2
    sibling = y * 2 + (1 - core)

    barrier = pltpu.get_barrier_semaphore()
    for d in range(1, 8):
        pl.semaphore_signal(barrier, inc=1, device_id=(ctx, (head + d) % 8), device_id_type=MESH)

    def greet_x(later, carry):
        pl.semaphore_signal(barrier, inc=1, device_id=(later * NZ + z, head), device_id_type=MESH)
        return carry

    def greet_z(later, carry):
        pl.semaphore_signal(barrier, inc=1, device_id=(x * NZ + later, head), device_id_type=MESH)
        return carry

    lax.fori_loop(x + 1, NX, greet_x, 0)
    lax.fori_loop(z + 1, NZ, greet_z, 0)
    for a in range(4):
        pltpu.make_async_copy(inputs[a], own.at[a], own_sem).start()
    pl.semaphore_wait(barrier, 7 + x + z)

    def answer_x(earlier, carry):
        pl.semaphore_signal(up_sem, inc=1, device_id=(earlier * NZ + z, head), device_id_type=MESH)
        return carry

    def answer_z(earlier, carry):
        pl.semaphore_signal(up_sem, inc=1, device_id=(x * NZ + earlier, head), device_id_type=MESH)
        return carry

    lax.fori_loop(0, x, answer_x, 0)
    lax.fori_loop(0, z, answer_z, 0)

    def raw(h, dy, dc, a):
        to = (y + dy) % NY * 2 + (core + dc) % 2
        return pltpu.make_async_remote_copy(
            src_ref=inputs[a].at[:, pl.ds(pl.multiple_of(to * 512 + h * HD, HD), HD)],
            dst_ref=recv.at[a, h, pl.ds(pl.multiple_of(head * HD, HD), HD), :],
            send_sem=raw_send,
            recv_sem=raw_recv.at[h, (NY - dy) % NY],
            device_id=(ctx, to),
            device_id_type=MESH,
        )

    peers = [(0, 1)] + [(dy, dc) for dy in (1, 3, 2) for dc in range(2)]

    def keep(h, arrays):
        for a in arrays:
            pltpu.make_async_copy(
                inputs[a].at[:, pl.ds(pl.multiple_of(head * 512 + h * HD, HD), HD)],
                recv.at[a, h, pl.ds(pl.multiple_of(head * HD, HD), HD), :],
                raw_recv.at[h, 0],
            ).start()

    def send(h, arrays):
        for dy, dc in peers:
            for a in arrays:
                raw(h, dy, dc, a).start()

    keep(0, range(4))
    send(0, range(4))

    up = 1 + 2 * core
    down = 3 - 2 * core
    for a in range(4):
        pltpu.make_async_copy(inputs[a], own.at[a], own_sem).wait()

    def partial(dest, st):
        cols = pl.ds(pl.multiple_of(dest * 512 + 256 + st // 2 * HD, HD), HD)
        if st % 2 == 0:
            return mm(own[1, :, cols], own[2, :, cols], 0, 0)
        return mm(own[0, :, cols], own[3, :, cols], 0, 0)

    for n, dy in enumerate((2, up, down, 0)):
        for st in range(4):
            sib_out[n, st] = partial((y + dy) % NY * 2 + 1 - core, st)
        place = (0, 2, 1, 3)[n]
        pltpu.make_async_remote_copy(
            src_ref=sib_out.at[n],
            dst_ref=sib_in.at[place],
            send_sem=sib_send,
            recv_sem=sib_recv.at[place],
            device_id=(ctx, sibling),
            device_id_type=MESH,
        ).start()

    def send_early(n, dy):
        pltpu.make_async_remote_copy(
            src_ref=early_out.at[n],
            dst_ref=early_in.at[n],
            send_sem=early_send,
            recv_sem=early_recv.at[n],
            device_id=(ctx, (y + dy) % NY * 2 + core),
            device_id_type=MESH,
        ).start()

    for n, dy in ((0, 2), (2, down), (1, up), (3, 0)):
        pltpu.make_async_copy(sib_in.at[n], sib_in.at[n], sib_recv.at[n]).wait()
        for st in range(4):
            both = partial((y + dy) % NY * 2 + core, st) + sib_in[n, st]
            if n == 3:
                subs[2 + st // 2, y, st % 2] = both
            elif n == 1:
                onward[st] = both
            else:
                early_out[n, st] = both.astype(BF16)
        if n == 0:
            send_early(0, up)
        if n == 2:
            send_early(2, down)

    keep(1, range(4))
    send(1, (1, 2))
    pltpu.make_async_copy(early_in.at[0], early_in.at[0], early_recv.at[0]).wait()
    for st in range(4):
        early_out[1, st] = (onward[st] + early_in[0, st].astype(F32)).astype(BF16)
    send_early(1, up)
    send(1, (0, 3))

    def send_rest(h, carry):
        keep(h, range(4))
        send(h, range(4))
        return carry

    lax.fori_loop(2, 4, send_rest, 0)

    row = lax.broadcasted_iota(jnp.int32, (SUB, SUB), 0)
    col = lax.broadcasted_iota(jnp.int32, (SUB, SUB), 1)
    causal = row >= col

    def load(h, i):
        return tuple(recv[a, h, pl.ds(pl.multiple_of(i * SUB, SUB), SUB), :] for a in range(4))

    def within(qs, ks, vs, gs):
        attn = jnp.where(causal, mm(qs, ks, 1, 1), 0.0).astype(BF16)
        back = jnp.where(causal, mm(gs, vs, 1, 1), 0.0).astype(BF16)
        return mm(attn, vs, 1, 0), mm(back, ks, 1, 0), mm(back, qs, 0, 0), mm(attn, gs, 0, 0)

    def across(h, i, qs, ks, vs, gs):
        pre, suf = entering[h, 0:HD, :], entering[h, HD : 2 * HD, :]
        pre_in, suf_in = inner[h, i, 0], inner[h, i, 1]

        def twice(rows):
            return jnp.concatenate([rows, rows], axis=1)

        pre_rows, pre_cols = jnp.concatenate([pre, pre_in], axis=0), jnp.concatenate([pre, pre_in], axis=1)
        suf_rows, suf_cols = jnp.concatenate([suf, suf_in], axis=0), jnp.concatenate([suf, suf_in], axis=1)
        return (
            mm(twice(qs), pre_rows, 1, 0),
            mm(twice(gs), pre_cols, 1, 1),
            mm(twice(vs), suf_cols, 1, 1),
            mm(twice(ks), suf_rows, 1, 0),
        )

    def arrive(h, j):
        i = (y + j) % NY
        landed = recv.at[:, h, pl.ds(pl.multiple_of(i * SUB, SUB), SUB), :]
        pltpu.make_async_copy(landed, landed, raw_recv.at[h, j]).wait()
        return i

    def first_heads(h, low, high):
        def one(m, carry):
            i = arrive(h, m + m // 2 - 2 * (m // 3))
            parts = load(h, i)
            qs, ks, vs, gs = parts
            subs[h, i, 0] = mm(ks, vs, 0, 0)
            subs[h, i, 1] = mm(qs, gs, 0, 0)
            rows = pl.ds(pl.multiple_of(i * SUB, SUB), SUB)
            for n, part in enumerate(within(*parts)):
                acc[n, h, rows, :] = part
            return carry

        lax.fori_loop(low, high, one, 0)

    def store(h, i, values):
        rows = pl.ds(pl.multiple_of(i * SUB, SUB), SUB)
        for ref, value in zip(outputs, values):
            ref[rows, pl.ds(h * HD, HD)] = (value * scale).astype(BF16)

    def whole(h, i):
        parts = load(h, i)
        far = across(h, i, *parts)
        store(h, i, [near + more for near, more in zip(within(*parts), far)])

    def last_heads(h):
        for j in (0, 1, 3):
            arrive(h, j)
        before = (y + down) % NY
        qs, ks, vs, gs = load(h, before)
        for st, state in enumerate((mm(ks, vs, 0, 0), mm(qs, gs, 0, 0))):
            place = 2 * (h - 2) + st
            subs[h, (y + up) % NY, st] = early_in[2, place].astype(F32)
            subs[h, before, st] = state
            subs[h, (y + 2) % NY, st] = early_in[1, place].astype(F32) - state
        inner_states(h)

        def one(m, carry):
            whole(h, (y + m + m // 2) % NY)
            return carry

        lax.fori_loop(0, 3, one, 0)

    def finish(h):
        def one(i, carry):
            rows = pl.ds(pl.multiple_of(i * SUB, SUB), SUB)
            far = across(h, i, *load(h, i))
            store(h, i, [acc[n, h, rows, :] + more for n, more in enumerate(far)])
            return carry

        lax.fori_loop(0, NY, one, 0)

    def inner_states(h):
        for st in range(2):
            state = jnp.zeros((HD, HD), F32)
            for i in range(NY) if st == 0 else reversed(range(NY)):
                inner[h, i, st] = state.astype(BF16)
                state = state + subs[h, i, st]

    def block_states(h):
        for st in range(2):
            if h < 2:
                total = subs[h, 0, st] + subs[h, 1, st] + subs[h, 2, st] + subs[h, 3, st]
            else:
                place = 2 * (h - 2) + st
                total = subs[h, y, st] + early_in[1, place].astype(F32) + early_in[2, place].astype(F32)
            states[h, pl.ds(st * HD, HD), :] = total.astype(BF16)

    ahead = z < NZ // 2
    far_first = (4, 3, 5, 2, 6, 1, 7)

    def slice_of(place):
        return pl.ds(pl.multiple_of(place * SLICE, SLICE), SLICE)

    def scan_one(h):
        pin[h, z] = states[h, slice_of(z), :]
        for dz in far_first:
            to = (z + dz) % NZ
            pltpu.make_async_remote_copy(
                src_ref=states.at[h, slice_of(to), :],
                dst_ref=pin.at[h, z],
                send_sem=scan_send.at[h, 0],
                recv_sem=scan_recv.at[h, 0],
                device_id=(x * NZ + to, head),
                device_id_type=MESH,
            ).start()

    def scan_two(h):
        landed = pin.at[h, pl.ds(0, NZ - 1)]
        pltpu.make_async_copy(landed, landed, scan_recv.at[h, 0]).wait()
        total = pin[h, 0].astype(F32)
        for i in range(1, NZ):
            total = total + pin[h, i].astype(F32)
        totals[h, x] = total
        for dx in (2, 1, 3):
            pltpu.make_async_remote_copy(
                src_ref=totals.at[h, x],
                dst_ref=totals.at[h, x],
                send_sem=scan_send.at[h, 1],
                recv_sem=scan_recv.at[h, 1],
                device_id=((x + dx) % NX * NZ + z, head),
                device_id_type=MESH,
            ).start()

    def scan_three(h):
        landed = totals.at[h, pl.ds(0, NX - 1)]
        pltpu.make_async_copy(landed, landed, scan_recv.at[h, 1]).wait()
        base = jnp.zeros((SLICE, HD), F32)
        for i in range(NX):
            counts = jnp.logical_or(jnp.logical_and(ahead, i < x), jnp.logical_and(jnp.logical_not(ahead), i > x))
            base = base + jnp.where(counts, totals[h, i], 0.0)
        total = totals[h, x]
        before = jnp.zeros((SLICE, HD), F32)
        for i in range(NZ):
            mine = pin[h, i].astype(F32)
            part = jnp.where(ahead, before, total - before - mine)
            pout[h, i] = (base + part).astype(BF16)
            before = before + mine
        entering[h, slice_of(z), :] = pout[h, z]
        for dz in far_first:
            to = (z + dz) % NZ
            pltpu.make_async_remote_copy(
                src_ref=pout.at[h, to],
                dst_ref=entering.at[h, slice_of(z), :],
                send_sem=scan_send.at[h, 2],
                recv_sem=scan_recv.at[h, 2],
                device_id=(x * NZ + to, head),
                device_id_type=MESH,
            ).start()

    def scan_end(h):
        landed = pout.at[h, pl.ds(0, NZ - 1)]
        pltpu.make_async_copy(landed, landed, scan_recv.at[h, 2]).wait()

    first_heads(0, 0, 4)
    block_states(0)
    later = NX - 1 - x + NZ - 1 - z

    @pl.when(later > 0)
    def _():
        pl.semaphore_wait(up_sem, later)

    scan_one(0)
    for n in (1, 2):
        pltpu.make_async_copy(early_in.at[n], early_in.at[n], early_recv.at[n]).wait()
    for h in (2, 3):
        block_states(h)
        scan_one(h)
    first_heads(1, 0, 3)
    for h in (0, 2, 3):
        scan_two(h)
    first_heads(1, 3, 4)
    block_states(1)
    scan_one(1)
    for h in (0, 2, 3):
        scan_three(h)
    inner_states(0)
    inner_states(1)
    scan_two(1)
    scan_three(1)
    scan_end(2)
    last_heads(2)
    whole(2, arrive(2, 2))
    scan_end(3)
    scan_end(0)
    finish(0)
    scan_end(1)
    finish(1)
    last_heads(3)
    whole(3, arrive(3, 2))

    sent = recv.at[:, :, pl.ds(0, 896), :]
    pltpu.make_async_copy(sent, sent, raw_send).wait()
    pltpu.make_async_copy(sib_out, sib_out, sib_send).wait()
    sent = early_in
    pltpu.make_async_copy(sent, sent, early_send).wait()
    for n in range(4):
        sent = pout.at[n, pl.ds(0, NZ - 1)]
        pltpu.make_async_copy(sent, sent, scan_send.at[n, 0]).wait()
        pltpu.make_async_copy(sent, sent, scan_send.at[n, 2]).wait()
        sent = totals.at[n, pl.ds(0, NX - 1)]
        pltpu.make_async_copy(sent, sent, scan_send.at[n, 1]).wait()


def write_out(a, b, c, d, out_a, out_b, out_c, out_d, sem):
    pairs = ((a, out_a), (b, out_b), (c, out_c), (d, out_d))
    for src, dst in pairs:
        pltpu.make_async_copy(src, dst, sem).start()
    for src, dst in pairs:
        pltpu.make_async_copy(src, dst, sem).wait()


def on_device(queries, key_rows, value_rows, out_grad):
    def body(*refs):
        kernel(1.0 / math.sqrt(4194304), *refs)

    dma = pltpu.SemaphoreType.DMA
    results = pl.pallas_call(
        body,
        out_shape=[pltpu.VMEM((1024, 512), BF16)] * 4,
        in_specs=[pl.BlockSpec(memory_space=pl.ANY)] * 4,
        out_specs=[pl.BlockSpec(memory_space=pltpu.VMEM)] * 4,
        scratch_shapes=[
            pltpu.VMEM((4, 4, 1024, HD), BF16),
            pltpu.VMEM((4, 128, 4096), BF16),
            pltpu.VMEM((4, 2, 1024, HD), F32),
            pltpu.VMEM((4, 4, HD, HD), F32),
            pltpu.VMEM((4, 4, HD, HD), F32),
            pltpu.VMEM((3, 4, HD, HD), BF16),
            pltpu.VMEM((3, 4, HD, HD), BF16),
            pltpu.VMEM((4, HD, HD), F32),
            pltpu.VMEM((4, 4, 2, HD, HD), F32),
            pltpu.VMEM((4, 2 * HD, HD), BF16),
            pltpu.VMEM((4, NZ, SLICE, HD), BF16),
            pltpu.VMEM((4, NX, SLICE, HD), F32),
            pltpu.VMEM((4, NZ, SLICE, HD), BF16),
            pltpu.VMEM((4, 2 * HD, HD), BF16),
            pltpu.VMEM((4, 4, 2, HD, HD), BF16),
            dma,
            dma((4, 4)),
            dma,
            dma,
            dma((4,)),
            dma,
            dma((3,)),
            dma((4, 3)),
            dma((4, 3)),
            pltpu.SemaphoreType.REGULAR,
        ],
        compiler_params=pltpu.CompilerParams(
            collective_id=0, has_side_effects=True, vmem_limit_bytes=VMEM_LIMIT
        ),
        name="linear_attention",
    )(queries, key_rows, value_rows, out_grad)
    return pl.pallas_call(
        write_out,
        out_shape=[pltpu.HBM((1024, 512), BF16)] * 4,
        in_specs=[pl.BlockSpec(memory_space=pltpu.VMEM)] * 4,
        out_specs=[pl.BlockSpec(memory_space=pltpu.HBM)] * 4,
        scratch_shapes=[dma],
        compiler_params=pltpu.CompilerParams(vmem_limit_bytes=VMEM_LIMIT),
        name="write_out",
    )(*[pltpu.with_memory_space_constraint(result, pltpu.VMEM) for result in results])


def solution(mesh):
    return jax.shard_map(
        on_device,
        mesh=mesh,
        in_specs=(P(("ctx", "head"), None),) * 4,
        out_specs=(P("ctx", "head"),) * 4,
        check_vma=False,
    )
```

```python
import math

import jax
import jax.numpy as jnp
from jax import lax
from jax.experimental import pallas as pl
from jax.experimental.pallas import tpu as pltpu
from jax.sharding import PartitionSpec as P

HD = 128
NX, NZ, NY = 4, 8, 4
SUB = 256
SLICE = 2 * HD // NZ
VMEM_LIMIT = 58 * 2**20
MESH = pl.DeviceIdType.MESH
F32 = jnp.float32
BF16 = jnp.bfloat16


def mm(left, right, left_dim, right_dim):
    return lax.dot_general(
        left, right, (((left_dim,), (right_dim,)), ((), ())), preferred_element_type=F32
    )


def kernel(
    scale, q, k, v, g, o0, o1, o2, o3,
    recv, own, acc, sib_out, sib_in, early_out, early_in, onward, subs, states, pin, totals, pout,
    entering, inner, raw_send, raw_recv, own_sem, sib_send, sib_recv, early_send, early_recv,
    scan_send, scan_recv, up_sem, first_sem,
):
    inputs = (q, k, v, g)
    outputs = (o0, o1, o2, o3)
    ctx = lax.axis_index("ctx")
    head = lax.axis_index("head")
    x, z = ctx // NZ, ctx % NZ
    y, core = head // 2, head % 2
    sibling = y * 2 + (1 - core)

    barrier = pltpu.get_barrier_semaphore()

    @pl.when(head > 0)
    def _():
        for d in range(1, 8):
            pl.semaphore_signal(barrier, inc=1, device_id=(ctx, (head + d) % 8), device_id_type=MESH)


    def greet_x(later, carry):
        pl.semaphore_signal(barrier, inc=1, device_id=(later * NZ + z, head), device_id_type=MESH)
        return carry

    def greet_z(later, carry):
        pl.semaphore_signal(barrier, inc=1, device_id=(x * NZ + later, head), device_id_type=MESH)
        return carry

    lax.fori_loop(x + 1, NX, greet_x, 0)
    lax.fori_loop(z + 1, NZ, greet_z, 0)
    for a in range(4):
        pltpu.make_async_copy(inputs[a], own.at[a], own_sem).start()
    pl.semaphore_wait(barrier, 7 - (head + 7) // 8 + x + z)

    @pl.when(head == 0)
    def _():
        for d in range(1, 8):
            pl.semaphore_signal(first_sem, inc=1, device_id=(ctx, d), device_id_type=MESH)


    def answer_x(earlier, carry):
        pl.semaphore_signal(up_sem, inc=1, device_id=(earlier * NZ + z, head), device_id_type=MESH)
        return carry

    def answer_z(earlier, carry):
        pl.semaphore_signal(up_sem, inc=1, device_id=(x * NZ + earlier, head), device_id_type=MESH)
        return carry

    lax.fori_loop(0, x, answer_x, 0)
    lax.fori_loop(0, z, answer_z, 0)

    def sem_row(h, a):
        return 4 if isinstance(h, int) and h == 1 and a in (0, 3) else h

    def raw(h, dy, dc, a):
        to = (y + dy) % NY * 2 + (core + dc) % 2
        return pltpu.make_async_remote_copy(
            src_ref=inputs[a].at[:, pl.ds(pl.multiple_of(to * 512 + h * HD, HD), HD)],
            dst_ref=recv.at[a, h, pl.ds(pl.multiple_of(head * HD, HD), HD), :],
            send_sem=raw_send,
            recv_sem=raw_recv.at[sem_row(h, a), (NY - dy) % NY],
            device_id=(ctx, to),
            device_id_type=MESH,
        )

    peers = [(0, 1)] + [(dy, dc) for dy in (1, 3, 2) for dc in range(2)]

    def keep(h, arrays):
        for a in arrays:
            pltpu.make_async_copy(
                inputs[a].at[:, pl.ds(pl.multiple_of(head * 512 + h * HD, HD), HD)],
                recv.at[a, h, pl.ds(pl.multiple_of(head * HD, HD), HD), :],
                raw_recv.at[sem_row(h, a), 0],
            ).start()

    def send(h, arrays):
        for dy, dc in peers:
            for a in arrays:
                raw(h, dy, dc, a).start()

    def raw_to(h, ty, tc):
        to = ty * 2 + tc

        @pl.when(to != head)
        def _():
            for a in range(4):
                pltpu.make_async_remote_copy(
                    src_ref=inputs[a].at[:, pl.ds(pl.multiple_of(to * 512 + h * HD, HD), HD)],
                    dst_ref=recv.at[a, h, pl.ds(pl.multiple_of(head * HD, HD), HD), :],
                    send_sem=raw_send,
                    recv_sem=raw_recv.at[h, (y + NY - ty) % NY],
                    device_id=(ctx, to),
                    device_id_type=MESH,
                ).start()

    def send_last(h):
        for dy in (0, 1, 3, 2):
            for tc in (1, 0):
                raw_to(h, (y + dy) % NY, tc)

    keep(0, range(4))
    for dy, dc in peers:

        @pl.when((y + dy) % NY * 2 + (core + dc) % 2 > 0)
        def _():
            for a in range(4):
                raw(0, dy, dc, a).start()

    @pl.when(head > 0)
    def _():
        pl.semaphore_wait(first_sem, 1)
        raw_to(0, 0, 0)

    up = 1 + 2 * core
    down = 3 - 2 * core
    for a in range(4):
        pltpu.make_async_copy(inputs[a], own.at[a], own_sem).wait()

    def partial(dest, st):
        cols = pl.ds(pl.multiple_of(dest * 512 + 256 + st // 2 * HD, HD), HD)
        if st % 2 == 0:
            return mm(own[1, :, cols], own[2, :, cols], 0, 0)
        return mm(own[0, :, cols], own[3, :, cols], 0, 0)

    for n, dy in enumerate((2, up, down, 0)):
        for st in range(4):
            sib_out[n, st] = partial((y + dy) % NY * 2 + 1 - core, st)
        place = (0, 2, 1, 3)[n]
        pltpu.make_async_remote_copy(
            src_ref=sib_out.at[n],
            dst_ref=sib_in.at[place],
            send_sem=sib_send,
            recv_sem=sib_recv.at[place],
            device_id=(ctx, sibling),
            device_id_type=MESH,
        ).start()

    def send_early(n, dy):
        pltpu.make_async_remote_copy(
            src_ref=early_out.at[n],
            dst_ref=early_in.at[n],
            send_sem=early_send,
            recv_sem=early_recv.at[n],
            device_id=(ctx, (y + dy) % NY * 2 + core),
            device_id_type=MESH,
        ).start()

    for n, dy in ((0, 2), (2, down), (1, up), (3, 0)):
        pltpu.make_async_copy(sib_in.at[n], sib_in.at[n], sib_recv.at[n]).wait()
        for st in range(4):
            both = partial((y + dy) % NY * 2 + core, st) + sib_in[n, st]
            if n == 3:
                subs[2 + st // 2, y, st % 2] = both
            elif n == 1:
                onward[st] = both
            else:
                early_out[n, st] = both.astype(BF16)
        if n == 0:
            send_early(0, up)
        if n == 2:
            send_early(2, down)

    keep(1, range(4))
    send(1, (1, 2))
    pltpu.make_async_copy(early_in.at[0], early_in.at[0], early_recv.at[0]).wait()
    for st in range(4):
        early_out[1, st] = (onward[st] + early_in[0, st].astype(F32)).astype(BF16)
    send_early(1, up)
    send(1, (0, 3))

    def send_rest(h, carry):
        keep(h, range(4))
        send(h, range(4))
        return carry

    send_rest(2, 0)
    keep(3, range(4))
    send_last(3)

    row = lax.broadcasted_iota(jnp.int32, (SUB, SUB), 0)
    col = lax.broadcasted_iota(jnp.int32, (SUB, SUB), 1)
    causal = row >= col

    def load(h, i):
        return tuple(recv[a, h, pl.ds(pl.multiple_of(i * SUB, SUB), SUB), :] for a in range(4))

    def within(qs, ks, vs, gs):
        attn = jnp.where(causal, mm(qs, ks, 1, 1), 0.0).astype(BF16)
        back = jnp.where(causal, mm(gs, vs, 1, 1), 0.0).astype(BF16)
        return mm(attn, vs, 1, 0), mm(back, ks, 1, 0), mm(back, qs, 0, 0), mm(attn, gs, 0, 0)

    def across(h, i, qs, ks, vs, gs):
        pre, suf = entering[h, 0:HD, :], entering[h, HD : 2 * HD, :]
        pre_in, suf_in = inner[h, i, 0], inner[h, i, 1]

        def twice(rows):
            return jnp.concatenate([rows, rows], axis=1)

        pre_rows, pre_cols = jnp.concatenate([pre, pre_in], axis=0), jnp.concatenate([pre, pre_in], axis=1)
        suf_rows, suf_cols = jnp.concatenate([suf, suf_in], axis=0), jnp.concatenate([suf, suf_in], axis=1)
        return (
            mm(twice(qs), pre_rows, 1, 0),
            mm(twice(gs), pre_cols, 1, 1),
            mm(twice(vs), suf_cols, 1, 1),
            mm(twice(ks), suf_rows, 1, 0),
        )

    def arrive(h, j):
        i = (y + j) % NY
        landed = recv.at[:, h, pl.ds(pl.multiple_of(i * SUB, SUB), SUB), :]
        pltpu.make_async_copy(landed, landed, raw_recv.at[h, j]).wait()
        return i

    def arrive_half(row, j):
        i = (y + j) % NY
        landed = recv.at[pl.ds(0, 2), 1, pl.ds(pl.multiple_of(i * SUB, SUB), SUB), :]
        pltpu.make_async_copy(landed, landed, raw_recv.at[row, j]).wait()
        return i

    def near_parts(h, i, parts):
        rows = pl.ds(pl.multiple_of(i * SUB, SUB), SUB)
        for n, part in enumerate(within(*parts)):
            acc[n, h, rows, :] = part

    def head_0():
        def one(m, carry):
            i = arrive(0, m + m // 2 - 2 * (m // 3))
            parts = load(0, i)
            qs, ks, vs, gs = parts
            subs[0, i, 0] = mm(ks, vs, 0, 0)
            subs[0, i, 1] = mm(qs, gs, 0, 0)
            near_parts(0, i, parts)
            return carry

        lax.fori_loop(0, NY, one, 0)

    def head_1_keys():
        def one(m, carry):
            i = arrive_half(1, m + m // 2 - 2 * (m // 3))
            qs, ks, vs, gs = load(1, i)
            subs[1, i, 0] = mm(ks, vs, 0, 0)
            return carry

        lax.fori_loop(0, NY, one, 0)

    def head_1_queries(j):
        i = arrive_half(4, j)
        qs, ks, vs, gs = load(1, i)
        subs[1, i, 1] = mm(qs, gs, 0, 0)
        return i

    def store(h, i, values):
        rows = pl.ds(pl.multiple_of(i * SUB, SUB), SUB)
        for ref, value in zip(outputs, values):
            ref[rows, pl.ds(h * HD, HD)] = (value * scale).astype(BF16)

    def whole(h, i):
        parts = load(h, i)
        far = across(h, i, *parts)
        store(h, i, [close + more for close, more in zip(within(*parts), far)])

    def whole(h, j):
        i = arrive(h, j)
        parts = load(h, i)
        far = across(h, i, *parts)
        store(h, i, [close + more for close, more in zip(within(*parts), far)])

    def near(h, j):
        i = arrive(h, j)
        near_parts(h, i, load(h, i))

    def other_states(h):
        before = (y + down) % NY
        qs, ks, vs, gs = load(h, before)
        for st, state in enumerate((mm(ks, vs, 0, 0), mm(qs, gs, 0, 0))):
            place = 2 * (h - 2) + st
            subs[h, (y + up) % NY, st] = early_in[2, place].astype(F32)
            subs[h, before, st] = state
            subs[h, (y + 2) % NY, st] = early_in[1, place].astype(F32) - state
        inner_states(h)

    def far_parts(h, i):
        rows = pl.ds(pl.multiple_of(i * SUB, SUB), SUB)
        far = across(h, i, *load(h, i))
        store(h, i, [acc[n, h, rows, :] + more for n, more in enumerate(far)])

    def finish(h):
        def one(m, carry):
            far_parts(h, 2 * m)
            far_parts(h, 2 * m + 1)
            return carry

        lax.fori_loop(0, NY // 2, one, 0)

    def inner_states(h):
        for st in range(2):
            state = jnp.zeros((HD, HD), F32)
            for i in range(NY) if st == 0 else reversed(range(NY)):
                inner[h, i, st] = state.astype(BF16)
                state = state + subs[h, i, st]

    def block_states(h, sts=(0, 1)):
        for st in sts:
            if h < 2:
                total = subs[h, 0, st] + subs[h, 1, st] + subs[h, 2, st] + subs[h, 3, st]
            else:
                place = 2 * (h - 2) + st
                total = subs[h, y, st] + early_in[1, place].astype(F32) + early_in[2, place].astype(F32)
            states[h, pl.ds(st * HD, HD), :] = total.astype(BF16)

    far_first = (4, 3, 5, 2, 6, 1, 7)

    class Scan:
        def __init__(self, n, h, first, rows):
            self.n, self.h, self.first, self.size = n, h, first, rows // NZ
            self.ahead = (first + z * self.size) // HD == 0

        def slice_of(self, place):
            return pl.ds(pl.multiple_of(self.first + place * self.size, self.size), self.size)

        def part(self, ref, place):
            return ref.at[self.n, place, pl.ds(0, self.size), :]

        def send(self, phase, src, dst, to):
            pltpu.make_async_remote_copy(
                src_ref=src,
                dst_ref=dst,
                send_sem=scan_send.at[self.n, phase],
                recv_sem=scan_recv.at[self.n, phase],
                device_id=(to, head),
                device_id_type=MESH,
            ).start()

        def landed(self, phase, ref, count, sems):
            copies = ref.at[self.n, pl.ds(0, count), pl.ds(0, self.size), :]
            pltpu.make_async_copy(copies, copies, sems.at[self.n, phase]).wait()

        def one(self):
            self.part(pin, z)[...] = states[self.h, self.slice_of(z), :]
            for dz in far_first:
                to = (z + dz) % NZ
                self.send(0, states.at[self.h, self.slice_of(to), :], self.part(pin, z), x * NZ + to)

        def two(self):
            self.landed(0, pin, NZ - 1, scan_recv)
            total = self.part(pin, 0)[...].astype(F32)
            for i in range(1, NZ):
                total = total + self.part(pin, i)[...].astype(F32)
            self.part(totals, x)[...] = total
            for dx in (2, 1, 3):
                self.send(1, self.part(totals, x), self.part(totals, x), (x + dx) % NX * NZ + z)

        def three(self):
            self.landed(1, totals, NX - 1, scan_recv)
            base = jnp.zeros((self.size, HD), F32)
            for i in range(NX):
                counts = jnp.logical_or(
                    jnp.logical_and(self.ahead, i < x),
                    jnp.logical_and(jnp.logical_not(self.ahead), i > x),
                )
                base = base + jnp.where(counts, self.part(totals, i)[...], 0.0)
            total = self.part(totals, x)[...]
            before = jnp.zeros((self.size, HD), F32)
            for i in range(NZ):
                mine = self.part(pin, i)[...].astype(F32)
                inside = jnp.where(self.ahead, before, total - before - mine)
                self.part(pout, i)[...] = (base + inside).astype(BF16)
                before = before + mine
            entering[self.h, self.slice_of(z), :] = self.part(pout, z)[...]
            for dz in far_first:
                to = (z + dz) % NZ
                self.send(2, self.part(pout, to), entering.at[self.h, self.slice_of(z), :], x * NZ + to)

        def end(self):
            self.landed(2, pout, NZ - 1, scan_recv)

        def sent(self):
            self.landed(0, pout, NZ - 1, scan_send)
            self.landed(1, totals, NX - 1, scan_send)
            self.landed(2, pout, NZ - 1, scan_send)

    scan_0, scan_2, scan_3 = (Scan(n, n, 0, 2 * HD) for n in (0, 2, 3))
    scan_1_keys, scan_1_queries = Scan(1, 1, 0, HD), Scan(4, 1, HD, HD)

    head_0()
    block_states(0)
    later = NX - 1 - x + NZ - 1 - z

    @pl.when(later > 0)
    def _():
        pl.semaphore_wait(up_sem, later)

    scan_0.one()
    head_1_keys()
    block_states(1, (0,))
    scan_1_keys.one()
    for n in (1, 2):
        pltpu.make_async_copy(early_in.at[n], early_in.at[n], early_recv.at[n]).wait()
    for h, scan in ((2, scan_2), (3, scan_3)):
        block_states(h)
        scan.one()

    def most(m, carry):
        i = head_1_queries(m + m // 2)
        near_parts(1, i, load(1, i))
        return carry

    lax.fori_loop(0, 3, most, 0)
    first_scans = (scan_0, scan_1_keys, scan_2, scan_3)
    for scan in first_scans:
        scan.two()
    last = head_1_queries(2)
    block_states(1, (1,))
    scan_1_queries.one()
    for scan in first_scans:
        scan.three()
    near_parts(1, last, load(1, last))
    inner_states(0)
    inner_states(1)
    near(2, 0)
    scan_1_queries.two()
    near(2, 1)
    near(2, 3)
    other_states(2)
    scan_1_queries.three()
    near(2, 2)
    scan_2.end()
    finish(2)
    scan_0.end()
    finish(0)
    near(3, 0)
    scan_3.end()
    arrive(3, 1)
    arrive(3, 3)
    other_states(3)
    far_parts(3, y)
    for j in (1, 3):
        i = (y + j) % NY
        parts = load(3, i)
        far = across(3, i, *parts)
        store(3, i, [close + more for close, more in zip(within(*parts), far)])
    scan_1_keys.end()
    scan_1_queries.end()
    finish(1)
    whole(3, 2)

    sent = recv.at[:, :, pl.ds(0, 896), :]
    pltpu.make_async_copy(sent, sent, raw_send).wait()
    pltpu.make_async_copy(sib_out, sib_out, sib_send).wait()
    sent = early_in
    pltpu.make_async_copy(sent, sent, early_send).wait()
    for scan in first_scans + (scan_1_queries,):
        scan.sent()


def write_out(a, b, c, d, out_a, out_b, out_c, out_d, sem):
    pairs = ((a, out_a), (b, out_b), (c, out_c), (d, out_d))
    for src, dst in pairs:
        pltpu.make_async_copy(src, dst, sem).start()
    for src, dst in pairs:
        pltpu.make_async_copy(src, dst, sem).wait()


def on_device(queries, key_rows, value_rows, out_grad):
    def body(*refs):
        kernel(1.0 / math.sqrt(4194304), *refs)

    dma = pltpu.SemaphoreType.DMA
    results = pl.pallas_call(
        body,
        out_shape=[pltpu.VMEM((1024, 512), BF16)] * 4,
        in_specs=[pl.BlockSpec(memory_space=pl.ANY)] * 4,
        out_specs=[pl.BlockSpec(memory_space=pltpu.VMEM)] * 4,
        scratch_shapes=[
            pltpu.VMEM((4, 4, 1024, HD), BF16),
            pltpu.VMEM((4, 128, 4096), BF16),
            pltpu.VMEM((4, 4, 1024, HD), F32),
            pltpu.VMEM((4, 4, HD, HD), F32),
            pltpu.VMEM((4, 4, HD, HD), F32),
            pltpu.VMEM((3, 4, HD, HD), BF16),
            pltpu.VMEM((3, 4, HD, HD), BF16),
            pltpu.VMEM((4, HD, HD), F32),
            pltpu.VMEM((4, 4, 2, HD, HD), F32),
            pltpu.VMEM((4, 2 * HD, HD), BF16),
            pltpu.VMEM((5, NZ, SLICE, HD), BF16),
            pltpu.VMEM((5, NX, SLICE, HD), F32),
            pltpu.VMEM((5, NZ, SLICE, HD), BF16),
            pltpu.VMEM((4, 2 * HD, HD), BF16),
            pltpu.VMEM((4, 4, 2, HD, HD), BF16),
            dma,
            dma((5, 4)),
            dma,
            dma,
            dma((4,)),
            dma,
            dma((3,)),
            dma((5, 3)),
            dma((5, 3)),
            pltpu.SemaphoreType.REGULAR,
            pltpu.SemaphoreType.REGULAR,
        ],
        compiler_params=pltpu.CompilerParams(
            collective_id=0, has_side_effects=True, vmem_limit_bytes=VMEM_LIMIT
        ),
        name="linear_attention",
    )(queries, key_rows, value_rows, out_grad)
    return pl.pallas_call(
        write_out,
        out_shape=[pltpu.HBM((1024, 512), BF16)] * 4,
        in_specs=[pl.BlockSpec(memory_space=pltpu.VMEM)] * 4,
        out_specs=[pl.BlockSpec(memory_space=pltpu.HBM)] * 4,
        scratch_shapes=[dma],
        compiler_params=pltpu.CompilerParams(vmem_limit_bytes=VMEM_LIMIT),
        name="write_out",
    )(*[pltpu.with_memory_space_constraint(result, pltpu.VMEM) for result in results])


def solution(mesh):
    return jax.shard_map(
        on_device,
        mesh=mesh,
        in_specs=(P(("ctx", "head"), None),) * 4,
        out_specs=(P("ctx", "head"),) * 4,
        check_vma=False,
    )
```

```python
import math

import jax
import jax.numpy as jnp
from jax import lax
from jax.experimental import pallas as pl
from jax.experimental.pallas import tpu as pltpu
from jax.sharding import PartitionSpec as P

HD = 128
NX, NZ, NY = 4, 8, 4
SUB = 256
SLICE = 2 * HD // NZ
VMEM_LIMIT = 58 * 2**20
MESH = pl.DeviceIdType.MESH
F32 = jnp.float32
BF16 = jnp.bfloat16


def mm(left, right, left_dim, right_dim):
    return lax.dot_general(
        left, right, (((left_dim,), (right_dim,)), ((), ())), preferred_element_type=F32
    )


def within(qs, ks, vs, gs):
    row = lax.broadcasted_iota(jnp.int32, (SUB, SUB), 0)
    col = lax.broadcasted_iota(jnp.int32, (SUB, SUB), 1)
    attn = jnp.where(row >= col, mm(qs, ks, 1, 1), 0.0).astype(BF16)
    back = jnp.where(row >= col, mm(gs, vs, 1, 1), 0.0).astype(BF16)
    return mm(attn, vs, 1, 0), mm(back, ks, 1, 0), mm(back, qs, 0, 0), mm(attn, gs, 0, 0)


def with_states(parts, pre, suf, pre_in, suf_in):
    qs, ks, vs, gs = (jnp.concatenate([rows, rows], axis=1) for rows in parts)
    pre_rows, pre_cols = jnp.concatenate([pre, pre_in], axis=0), jnp.concatenate([pre, pre_in], axis=1)
    suf_rows, suf_cols = jnp.concatenate([suf, suf_in], axis=0), jnp.concatenate([suf, suf_in], axis=1)
    return mm(qs, pre_rows, 1, 0), mm(gs, pre_cols, 1, 1), mm(vs, suf_cols, 1, 1), mm(ks, suf_rows, 1, 0)


def kernel(
    scale, q, k, v, g, o0, o1, o2, o3, last_raw, last_states,
    recv, own, acc, sib_out, sib_in, early_out, early_in, onward, subs, states, pin, totals, pout,
    entering, inner, raw_send, raw_recv, own_sem, sib_send, sib_recv, early_send, early_recv,
    scan_send, scan_recv, up_sem, first_sem,
):
    inputs = (q, k, v, g)
    outputs = (o0, o1, o2, o3)
    ctx = lax.axis_index("ctx")
    head = lax.axis_index("head")
    x, z = ctx // NZ, ctx % NZ
    y, core = head // 2, head % 2
    sibling = y * 2 + (1 - core)

    barrier = pltpu.get_barrier_semaphore()

    @pl.when(head > 0)
    def _():
        for d in range(1, 8):
            pl.semaphore_signal(barrier, inc=1, device_id=(ctx, (head + d) % 8), device_id_type=MESH)


    def greet_x(later, carry):
        pl.semaphore_signal(barrier, inc=1, device_id=(later * NZ + z, head), device_id_type=MESH)
        return carry

    def greet_z(later, carry):
        pl.semaphore_signal(barrier, inc=1, device_id=(x * NZ + later, head), device_id_type=MESH)
        return carry

    lax.fori_loop(x + 1, NX, greet_x, 0)
    lax.fori_loop(z + 1, NZ, greet_z, 0)
    for a in range(4):
        pltpu.make_async_copy(inputs[a], own.at[a], own_sem).start()
    pl.semaphore_wait(barrier, 7 - (head + 7) // 8 + x + z)

    @pl.when(head == 0)
    def _():
        for d in range(1, 8):
            pl.semaphore_signal(first_sem, inc=1, device_id=(ctx, d), device_id_type=MESH)


    def answer_x(earlier, carry):
        pl.semaphore_signal(up_sem, inc=1, device_id=(earlier * NZ + z, head), device_id_type=MESH)
        return carry

    def answer_z(earlier, carry):
        pl.semaphore_signal(up_sem, inc=1, device_id=(x * NZ + earlier, head), device_id_type=MESH)
        return carry

    lax.fori_loop(0, x, answer_x, 0)
    lax.fori_loop(0, z, answer_z, 0)

    def sem_row(h, a):
        return 4 if isinstance(h, int) and h == 1 and a in (0, 3) else h

    def raw(h, dy, dc, a):
        to = (y + dy) % NY * 2 + (core + dc) % 2
        return pltpu.make_async_remote_copy(
            src_ref=inputs[a].at[:, pl.ds(pl.multiple_of(to * 512 + h * HD, HD), HD)],
            dst_ref=recv.at[a, h, pl.ds(pl.multiple_of(head * HD, HD), HD), :],
            send_sem=raw_send,
            recv_sem=raw_recv.at[sem_row(h, a), (NY - dy) % NY],
            device_id=(ctx, to),
            device_id_type=MESH,
        )

    peers = [(0, 1)] + [(dy, dc) for dy in (1, 3, 2) for dc in range(2)]

    def keep(h, arrays):
        for a in arrays:
            pltpu.make_async_copy(
                inputs[a].at[:, pl.ds(pl.multiple_of(head * 512 + h * HD, HD), HD)],
                recv.at[a, h, pl.ds(pl.multiple_of(head * HD, HD), HD), :],
                raw_recv.at[sem_row(h, a), 0],
            ).start()

    def send(h, arrays):
        for dy, dc in peers:
            for a in arrays:
                raw(h, dy, dc, a).start()

    def raw_to(h, ty, tc, apart=False):
        to = ty * 2 + tc

        @pl.when(to != head)
        def _():
            for a in range(4):
                rows = recv.at[a, h, pl.ds(pl.multiple_of(head * HD, HD), HD), :]
                if apart:
                    rows = last_raw.at[a, pl.ds(pl.multiple_of(core * HD, HD), HD), :]
                pltpu.make_async_remote_copy(
                    src_ref=inputs[a].at[:, pl.ds(pl.multiple_of(to * 512 + h * HD, HD), HD)],
                    dst_ref=rows,
                    send_sem=raw_send,
                    recv_sem=raw_recv.at[h, (y + NY - ty) % NY],
                    device_id=(ctx, to),
                    device_id_type=MESH,
                ).start()

    def send_last(h):
        for dy in (0, 1, 3, 2):
            for tc in (1, 0):
                raw_to(h, (y + dy) % NY, tc, dy == 2)

    keep(0, range(4))
    for dy, dc in peers:

        @pl.when((y + dy) % NY * 2 + (core + dc) % 2 > 0)
        def _():
            for a in range(4):
                raw(0, dy, dc, a).start()

    @pl.when(head > 0)
    def _():
        pl.semaphore_wait(first_sem, 1)
        raw_to(0, 0, 0)

    up = 1 + 2 * core
    down = 3 - 2 * core
    for a in range(4):
        pltpu.make_async_copy(inputs[a], own.at[a], own_sem).wait()

    def partial(dest, st):
        cols = pl.ds(pl.multiple_of(dest * 512 + 256 + st // 2 * HD, HD), HD)
        if st % 2 == 0:
            return mm(own[1, :, cols], own[2, :, cols], 0, 0)
        return mm(own[0, :, cols], own[3, :, cols], 0, 0)

    for n, dy in enumerate((2, up, down, 0)):
        for st in range(4):
            sib_out[n, st] = partial((y + dy) % NY * 2 + 1 - core, st)
        place = (0, 2, 1, 3)[n]
        pltpu.make_async_remote_copy(
            src_ref=sib_out.at[n],
            dst_ref=sib_in.at[place],
            send_sem=sib_send,
            recv_sem=sib_recv.at[place],
            device_id=(ctx, sibling),
            device_id_type=MESH,
        ).start()

    def send_early(n, dy):
        pltpu.make_async_remote_copy(
            src_ref=early_out.at[n],
            dst_ref=early_in.at[n],
            send_sem=early_send,
            recv_sem=early_recv.at[n],
            device_id=(ctx, (y + dy) % NY * 2 + core),
            device_id_type=MESH,
        ).start()

    for n, dy in ((0, 2), (2, down), (1, up), (3, 0)):
        pltpu.make_async_copy(sib_in.at[n], sib_in.at[n], sib_recv.at[n]).wait()
        for st in range(4):
            both = partial((y + dy) % NY * 2 + core, st) + sib_in[n, st]
            if n == 3:
                subs[2 + st // 2, y, st % 2] = both
            elif n == 1:
                onward[st] = both
            else:
                early_out[n, st] = both.astype(BF16)
        if n == 0:
            send_early(0, up)
        if n == 2:
            send_early(2, down)

    keep(1, range(4))
    send(1, (1, 2))
    pltpu.make_async_copy(early_in.at[0], early_in.at[0], early_recv.at[0]).wait()
    for st in range(4):
        early_out[1, st] = (onward[st] + early_in[0, st].astype(F32)).astype(BF16)
    send_early(1, up)
    send(1, (0, 3))

    def send_rest(h, carry):
        keep(h, range(4))
        send(h, range(4))
        return carry

    send_rest(2, 0)
    keep(3, range(4))
    send_last(3)

    def load(h, i):
        return tuple(recv[a, h, pl.ds(pl.multiple_of(i * SUB, SUB), SUB), :] for a in range(4))

    def across(h, i, parts):
        return with_states(parts, entering[h, 0:HD, :], entering[h, HD : 2 * HD, :], inner[h, i, 0], inner[h, i, 1])

    def arrive(h, j):
        i = (y + j) % NY
        landed = recv.at[:, h, pl.ds(pl.multiple_of(i * SUB, SUB), SUB), :]
        pltpu.make_async_copy(landed, landed, raw_recv.at[h, j]).wait()
        return i

    def arrive_half(row, j):
        i = (y + j) % NY
        landed = recv.at[pl.ds(0, 2), 1, pl.ds(pl.multiple_of(i * SUB, SUB), SUB), :]
        pltpu.make_async_copy(landed, landed, raw_recv.at[row, j]).wait()
        return i

    def near_parts(h, i, parts):
        rows = pl.ds(pl.multiple_of(i * SUB, SUB), SUB)
        for n, part in enumerate(within(*parts)):
            acc[n, h, rows, :] = part

    def head_0():
        def one(m, carry):
            i = arrive(0, m + m // 2 - 2 * (m // 3))
            parts = load(0, i)
            qs, ks, vs, gs = parts
            subs[0, i, 0] = mm(ks, vs, 0, 0)
            subs[0, i, 1] = mm(qs, gs, 0, 0)
            near_parts(0, i, parts)
            return carry

        lax.fori_loop(0, NY, one, 0)

    def head_1_keys():
        def one(m, carry):
            i = arrive_half(1, m + m // 2 - 2 * (m // 3))
            qs, ks, vs, gs = load(1, i)
            subs[1, i, 0] = mm(ks, vs, 0, 0)
            return carry

        lax.fori_loop(0, NY, one, 0)

    def head_1_queries(j):
        i = arrive_half(4, j)
        qs, ks, vs, gs = load(1, i)
        subs[1, i, 1] = mm(qs, gs, 0, 0)
        return i

    def store(h, i, values):
        rows = pl.ds(pl.multiple_of(i * SUB, SUB), SUB)
        for ref, value in zip(outputs, values):
            ref[rows, pl.ds(h * HD, HD)] = (value * scale).astype(BF16)

    def whole(h, i):
        parts = load(h, i)
        far = across(h, i, parts)
        store(h, i, [close + more for close, more in zip(within(*parts), far)])

    def near(h, j):
        i = arrive(h, j)
        near_parts(h, i, load(h, i))

    def other_states(h):
        before = (y + down) % NY
        qs, ks, vs, gs = load(h, before)
        for st, state in enumerate((mm(ks, vs, 0, 0), mm(qs, gs, 0, 0))):
            place = 2 * (h - 2) + st
            subs[h, (y + up) % NY, st] = early_in[2, place].astype(F32)
            subs[h, before, st] = state
            subs[h, (y + 2) % NY, st] = early_in[1, place].astype(F32) - state
        inner_states(h)

    def far_parts(h, i):
        rows = pl.ds(pl.multiple_of(i * SUB, SUB), SUB)
        far = across(h, i, load(h, i))
        store(h, i, [acc[n, h, rows, :] + more for n, more in enumerate(far)])

    def finish(h):
        def one(m, carry):
            far_parts(h, 2 * m)
            far_parts(h, 2 * m + 1)
            return carry

        lax.fori_loop(0, NY // 2, one, 0)

    def inner_states(h):
        for st in range(2):
            state = jnp.zeros((HD, HD), F32)
            for i in range(NY) if st == 0 else reversed(range(NY)):
                inner[h, i, st] = state.astype(BF16)
                state = state + subs[h, i, st]

    def block_states(h, sts=(0, 1)):
        for st in sts:
            if h < 2:
                total = subs[h, 0, st] + subs[h, 1, st] + subs[h, 2, st] + subs[h, 3, st]
            else:
                place = 2 * (h - 2) + st
                total = subs[h, y, st] + early_in[1, place].astype(F32) + early_in[2, place].astype(F32)
            states[h, pl.ds(st * HD, HD), :] = total.astype(BF16)

    far_first = (4, 3, 5, 2, 6, 1, 7)

    class Scan:
        def __init__(self, n, h, first, rows):
            self.n, self.h, self.first, self.size = n, h, first, rows // NZ
            self.ahead = (first + z * self.size) // HD == 0

        def slice_of(self, place):
            return pl.ds(pl.multiple_of(self.first + place * self.size, self.size), self.size)

        def part(self, ref, place):
            return ref.at[self.n, place, pl.ds(0, self.size), :]

        def send(self, phase, src, dst, to):
            pltpu.make_async_remote_copy(
                src_ref=src,
                dst_ref=dst,
                send_sem=scan_send.at[self.n, phase],
                recv_sem=scan_recv.at[self.n, phase],
                device_id=(to, head),
                device_id_type=MESH,
            ).start()

        def landed(self, phase, ref, count, sems):
            copies = ref.at[self.n, pl.ds(0, count), pl.ds(0, self.size), :]
            pltpu.make_async_copy(copies, copies, sems.at[self.n, phase]).wait()

        def one(self):
            self.part(pin, z)[...] = states[self.h, self.slice_of(z), :]
            for dz in far_first:
                to = (z + dz) % NZ
                self.send(0, states.at[self.h, self.slice_of(to), :], self.part(pin, z), x * NZ + to)

        def two(self):
            self.landed(0, pin, NZ - 1, scan_recv)
            total = self.part(pin, 0)[...].astype(F32)
            for i in range(1, NZ):
                total = total + self.part(pin, i)[...].astype(F32)
            self.part(totals, x)[...] = total
            for dx in (2, 1, 3):
                self.send(1, self.part(totals, x), self.part(totals, x), (x + dx) % NX * NZ + z)

        def three(self):
            self.landed(1, totals, NX - 1, scan_recv)
            base = jnp.zeros((self.size, HD), F32)
            for i in range(NX):
                counts = jnp.logical_or(
                    jnp.logical_and(self.ahead, i < x),
                    jnp.logical_and(jnp.logical_not(self.ahead), i > x),
                )
                base = base + jnp.where(counts, self.part(totals, i)[...], 0.0)
            total = self.part(totals, x)[...]
            before = jnp.zeros((self.size, HD), F32)
            for i in range(NZ):
                mine = self.part(pin, i)[...].astype(F32)
                inside = jnp.where(self.ahead, before, total - before - mine)
                self.part(pout, i)[...] = (base + inside).astype(BF16)
                before = before + mine
            entering[self.h, self.slice_of(z), :] = self.part(pout, z)[...]
            for dz in far_first:
                to = (z + dz) % NZ
                self.send(2, self.part(pout, to), entering.at[self.h, self.slice_of(z), :], x * NZ + to)

        def end(self):
            self.landed(2, pout, NZ - 1, scan_recv)

        def sent(self):
            self.landed(0, pout, NZ - 1, scan_send)
            self.landed(1, totals, NX - 1, scan_send)
            self.landed(2, pout, NZ - 1, scan_send)

    scan_0, scan_2, scan_3 = (Scan(n, n, 0, 2 * HD) for n in (0, 2, 3))
    scan_1_keys, scan_1_queries = Scan(1, 1, 0, HD), Scan(4, 1, HD, HD)

    head_0()
    block_states(0)
    later = NX - 1 - x + NZ - 1 - z

    @pl.when(later > 0)
    def _():
        pl.semaphore_wait(up_sem, later)

    scan_0.one()
    head_1_keys()
    block_states(1, (0,))
    scan_1_keys.one()
    for n in (1, 2):
        pltpu.make_async_copy(early_in.at[n], early_in.at[n], early_recv.at[n]).wait()
    for h, scan in ((2, scan_2), (3, scan_3)):
        block_states(h)
        scan.one()

    def most(m, carry):
        i = head_1_queries(m + m // 2)
        near_parts(1, i, load(1, i))
        return carry

    lax.fori_loop(0, 3, most, 0)
    first_scans = (scan_0, scan_1_keys, scan_2, scan_3)
    for scan in first_scans:
        scan.two()
    last = head_1_queries(2)
    block_states(1, (1,))
    scan_1_queries.one()
    for scan in first_scans:
        scan.three()
    near_parts(1, last, load(1, last))
    inner_states(0)
    inner_states(1)
    near(2, 0)
    scan_1_queries.two()
    near(2, 1)
    near(2, 3)
    other_states(2)
    scan_1_queries.three()
    near(2, 2)
    scan_2.end()
    finish(2)
    scan_0.end()
    finish(0)
    near(3, 0)
    scan_3.end()
    arrive(3, 1)
    arrive(3, 3)
    other_states(3)
    far_parts(3, y)
    for st in range(2):
        last_states[st] = entering[3, pl.ds(st * HD, HD), :]
        last_states[2 + st] = inner[3, (y + 2) % NY, st]
    for j in (1, 3):
        i = (y + j) % NY
        parts = load(3, i)
        far = across(3, i, parts)
        store(3, i, [close + more for close, more in zip(within(*parts), far)])
    scan_1_keys.end()
    scan_1_queries.end()
    finish(1)
    pltpu.make_async_copy(last_raw, last_raw, raw_recv.at[3, 2]).wait()

    sent = recv.at[:, :, pl.ds(0, 896), :]
    pltpu.make_async_copy(sent, sent, raw_send).wait()
    pltpu.make_async_copy(sib_out, sib_out, sib_send).wait()
    sent = early_in
    pltpu.make_async_copy(sent, sent, early_send).wait()
    for scan in first_scans + (scan_1_queries,):
        scan.sent()


def write_out(
    scale, a, b, c, d, last_raw, last_states, out_a, out_b, out_c, out_d, last, sem, last_sem
):
    place = (lax.axis_index("head") // 2 + 2) % NY

    def rows_of(i):
        return pl.ds(pl.multiple_of(i * SUB, SUB), SUB)

    most, rest = pl.ds(0, 3 * HD), pl.ds(3 * HD, HD)
    copies = []
    for src, dst in ((a, out_a), (b, out_b), (c, out_c), (d, out_d)):
        for n in range(1, NY):
            rows = rows_of((place + n) % NY)
            copies.append(pltpu.make_async_copy(src.at[rows, :], dst.at[rows, :], sem))
        rows = rows_of(place)
        copies.append(pltpu.make_async_copy(src.at[rows, most], dst.at[rows, most], sem))
    for copy in copies:
        copy.start()
    parts = tuple(last_raw[n] for n in range(4))
    far = with_states(parts, *(last_states[n] for n in range(4)))
    for n, (close, more, dst) in enumerate(zip(within(*parts), far, (out_a, out_b, out_c, out_d))):
        last[n] = ((close + more) * scale).astype(BF16)
        copies.append(pltpu.make_async_copy(last.at[n], dst.at[rows_of(place), rest], last_sem))
        copies[-1].start()
    for copy in copies:
        copy.wait()


def on_device(queries, key_rows, value_rows, out_grad):
    scale = 1.0 / math.sqrt(4194304)

    def body(*refs):
        kernel(scale, *refs)

    def write_body(*refs):
        write_out(scale, *refs)

    dma = pltpu.SemaphoreType.DMA
    results = pl.pallas_call(
        body,
        out_shape=[pltpu.VMEM((1024, 512), BF16)] * 4
        + [pltpu.VMEM((4, SUB, HD), BF16), pltpu.VMEM((4, HD, HD), BF16)],
        in_specs=[pl.BlockSpec(memory_space=pl.ANY)] * 4,
        out_specs=[pl.BlockSpec(memory_space=pltpu.VMEM)] * 6,
        scratch_shapes=[
            pltpu.VMEM((4, 4, 1024, HD), BF16),
            pltpu.VMEM((4, 128, 4096), BF16),
            pltpu.VMEM((4, 4, 1024, HD), F32),
            pltpu.VMEM((4, 4, HD, HD), F32),
            pltpu.VMEM((4, 4, HD, HD), F32),
            pltpu.VMEM((3, 4, HD, HD), BF16),
            pltpu.VMEM((3, 4, HD, HD), BF16),
            pltpu.VMEM((4, HD, HD), F32),
            pltpu.VMEM((4, 4, 2, HD, HD), F32),
            pltpu.VMEM((4, 2 * HD, HD), BF16),
            pltpu.VMEM((5, NZ, SLICE, HD), BF16),
            pltpu.VMEM((5, NX, SLICE, HD), F32),
            pltpu.VMEM((5, NZ, SLICE, HD), BF16),
            pltpu.VMEM((4, 2 * HD, HD), BF16),
            pltpu.VMEM((4, 4, 2, HD, HD), BF16),
            dma,
            dma((5, 4)),
            dma,
            dma,
            dma((4,)),
            dma,
            dma((3,)),
            dma((5, 3)),
            dma((5, 3)),
            pltpu.SemaphoreType.REGULAR,
            pltpu.SemaphoreType.REGULAR,
        ],
        compiler_params=pltpu.CompilerParams(
            collective_id=0, has_side_effects=True, vmem_limit_bytes=VMEM_LIMIT
        ),
        name="linear_attention",
    )(queries, key_rows, value_rows, out_grad)
    return pl.pallas_call(
        write_body,
        out_shape=[pltpu.HBM((1024, 512), BF16)] * 4,
        in_specs=[pl.BlockSpec(memory_space=pltpu.VMEM)] * 6,
        out_specs=[pl.BlockSpec(memory_space=pltpu.HBM)] * 4,
        scratch_shapes=[pltpu.VMEM((4, SUB, HD), BF16), dma, dma],
        compiler_params=pltpu.CompilerParams(vmem_limit_bytes=VMEM_LIMIT),
        name="write_out",
    )(*[pltpu.with_memory_space_constraint(result, pltpu.VMEM) for result in results])


def solution(mesh):
    return jax.shard_map(
        on_device,
        mesh=mesh,
        in_specs=(P(("ctx", "head"), None),) * 4,
        out_specs=(P("ctx", "head"),) * 4,
        check_vma=False,
    )
```
